32 devices in a mesh: seq: 16 (over z, x, core), head: 2 (over y).
Axes of the slice: x: 2, y: 2, z: 4, core: 2. Of those that a mesh axis runs over, the one named last changes fastest.
Arguments:
- queries: bfloat16 [16384, 1024], P('seq', 'head'), may hold values from -8 to 8
- keys: bfloat16 [16384, 1024], P('seq', 'head'), may hold values from -6 to 6
- values: bfloat16 [16384, 1024], P('seq', 'head'), may hold values from -6 to 6
- partners: int32 [256, 3], P('seq'), may hold values from 0 to 255, as said below
- out_weight: bfloat16 [1024, 1024], P('head'), may hold values from -0.1875 to 0.1875
- grad_out: bfloat16 [16384, 1024], P(('seq', 'head')), may hold values from -6 to 6
Outputs:
- mixed: bfloat16 [16384, 1024], P(('seq', 'head'))
- grad_queries: bfloat16 [16384, 1024], P('seq', 'head')
- grad_keys: bfloat16 [16384, 1024], P('seq', 'head')
- grad_values: bfloat16 [16384, 1024], P('seq', 'head')
- grad_weight: float32 [1024, 1024], P('head', 'seq')
The draws below stay inside these ranges and needn't reach their ends.
Inputs may be any that keep to these rules, and one draw needn't show every extreme that they name: `partners`: the 16 query blocks of one shard (rows 16 * d to 16 * d + 15) name at most 3 partner blocks, counted with repeats, among the blocks of any one shard (blocks 16 * s to 16 * s + 15); some pair of shards reaches 3 in every draw.
All inputs are finite; a program needn't handle non-finite values.
Results may differ from the reference program's by a relative error of at most 0.012.
The reference program's roundings to bfloat16 on the way count: a program that leaves them out, or rounds other values in their place, can miss the bound.
Values may be sent and summed in bfloat16 or wider, within the bound.
A program may use at most 192 MiB of HBM per device.

```python
import jax
import jax.numpy as jnp
from jax import lax

D = 1024
H = 16
DH = 64
BLK = 64
R = 3
SUMR = 16
NB_DEV = 16
SEQ = 16384
NBLK = 256
N_SEQ = 16


def draw_queries(key, part):
    key = jax.random.fold_in(key, 3)
    rows = 2.0 * jax.random.truncated_normal(key, -4.0, 4.0, (SEQ, D), jnp.float32)
    return rows.astype(jnp.bfloat16)


def draw_keys(key, part):
    key = jax.random.fold_in(key, 5)
    rows = jax.random.truncated_normal(key, -6.0, 6.0, (SEQ, D), jnp.float32)
    return rows.astype(jnp.bfloat16)


def draw_partners(key, part):
    key = jax.random.fold_in(key, 7)
    perm_key, inner_key = jax.random.split(key)

    def shuffle(subkey):
        return jax.random.permutation(subkey, N_SEQ)
    orders = jax.vmap(shuffle)(jax.random.split(perm_key, N_SEQ))
    request_ids = jnp.arange(NB_DEV * R)
    offsets = orders[:, request_ids % N_SEQ]
    owners = (jnp.arange(N_SEQ)[:, None] + offsets) % N_SEQ
    inside = jax.random.randint(inner_key, (N_SEQ, NB_DEV * R), 0, NB_DEV)
    blocks = owners * NB_DEV + inside
    return blocks.reshape(NBLK, R).astype(jnp.int32)


def with_spikes(values, key, source, target, shards_of, factor):
    def block_of(dim):
        return (jnp.arange(values.shape[dim]) // (values.shape[dim] // shards_of)).reshape((-1,) + (1,) * (values.ndim - 1 - dim))

    first = jax.random.permutation(key, shards_of)[block_of(target)]
    second = (block_of(target) + shards_of // 2) % shards_of
    return jnp.where((block_of(source) == first) | (block_of(source) == second), factor * values, values)


def level_of(key, extent, cuts, smallest, high):
    loudness, own = 1.0, jax.random.fold_in(key, 6)
    for position, blocks in cuts:
        draws = jnp.exp(jax.random.uniform(jax.random.fold_in(own, position), (blocks,), jnp.float32, smallest / len(cuts), high / len(cuts)))
        loudness = loudness * jnp.repeat(draws, extent[position] // blocks).reshape([-1 if axis == position else 1 for axis in range(len(extent))])
    return loudness


def scatter_about(rng, extent, spread, most, pieces=(), held_as=jnp.bfloat16):
    values = jax.random.normal(rng, extent, jnp.float32) * spread
    if len(pieces) > 0:
        values = level_of(rng, extent, pieces, -0.22, 0.18) * values
    return jnp.clip(values, min=-most, max=most).astype(held_as)


def heavy_noise(key, dims, deviation, most, cuts, heavy, kind=jnp.bfloat16):
    drawn = deviation * jax.random.normal(key, dims, jnp.float32)
    if cuts:
        drawn = drawn * level_of(key, dims, cuts, -0.22, 0.18)
    return jnp.clip(with_spikes(drawn, jax.random.fold_in(key, 3), *heavy), -most, most).astype(kind)


def setup_inputs(seed: int = 0) -> dict:
    seeds = jax.random.split(jax.random.key(seed), 7)
    queries = draw_queries(jax.random.fold_in(seeds[6], 71), 0)
    keys = draw_keys(jax.random.fold_in(seeds[6], 71), 0)
    values = scatter_about(seeds[2], (SEQ, D), 1.0, 6.0, ((0, 16), (1, 2)))
    partners = draw_partners(jax.random.fold_in(seeds[6], 71), 0)
    out_weight = scatter_about(seeds[4], (D, D), D ** -0.5, 0.1875, ((0, 2),))
    grad_out = heavy_noise(seeds[5], (SEQ, D), 1.0, 6.0, ((0, 32),), (0, 1, 32, 2.75))
    return {"queries": queries, "keys": keys, "values": values, "partners": partners, "out_weight": out_weight, "grad_out": grad_out}


def window_mask(nblocks):
    block_ids = jnp.arange(nblocks)
    left_ok = jnp.broadcast_to((block_ids > 0)[:, None], (nblocks, BLK))
    right_ok = jnp.broadcast_to((block_ids < nblocks - 1)[:, None], (nblocks, BLK))
    return jnp.concatenate([left_ok, jnp.ones((nblocks, BLK), bool), right_ok, jnp.ones((nblocks, R * BLK), bool)], 1)


def key_lists(head_rows, partners):
    nblocks = head_rows.shape[0]
    zero_block = jnp.zeros((1, BLK, DH), jnp.float32)
    padded = jnp.concatenate([zero_block, head_rows, zero_block], 0)
    window = jnp.concatenate([padded[:-2], padded[1:-1], padded[2:]], 1)
    chosen = head_rows[partners.reshape(-1)].reshape(nblocks, R * BLK, DH)
    return jnp.concatenate([window, chosen], 1)


def digest_blocks(head_rows):
    return head_rows.reshape(N_SEQ, -1, DH)[:, :SUMR].reshape(N_SEQ * SUMR, DH)


def probabilities(query_per_head, key_sequence, key_digest, allowed, score_scale):
    neighbour_blocks = jnp.einsum("gnm,gtm->gnt", query_per_head, key_sequence) * score_scale
    block_digest = jnp.einsum("mfp,jp->mfj", query_per_head, key_digest) * score_scale
    neighbour_blocks = jnp.where(allowed[:, None, :], neighbour_blocks, -1e30)
    highest = jnp.maximum(jnp.max(neighbour_blocks, -1), jnp.max(block_digest, -1))[..., None]
    near_exp = jnp.exp(neighbour_blocks - highest)
    far_exp = jnp.exp(block_digest - highest)
    totals = (jnp.sum(near_exp, -1) + jnp.sum(far_exp, -1))[..., None]
    return near_exp / totals, far_exp / totals


def to_bf16(values_f32):
    return lax.optimization_barrier(values_f32.astype(jnp.bfloat16)).astype(jnp.float32)


def attend_head(query_per_head, key_head, value_per_head, partners, allowed, score_scale):
    key_sequence = key_lists(key_head, partners)
    value_sequence = key_lists(value_per_head, partners)
    local_probs, distant_probs = probabilities(query_per_head, key_sequence, digest_blocks(key_head), allowed, score_scale)
    local_bias = to_bf16(local_probs)
    distant_bias = to_bf16(distant_probs)
    return jnp.einsum("teh,thz->tez", local_bias, value_sequence) + jnp.einsum("umj,jc->umc", distant_bias, digest_blocks(value_per_head))


def place_grads(list_grads, summary_grads, partners):
    nblocks = list_grads.shape[0]
    zero_block = jnp.zeros((1, BLK, DH), jnp.float32)
    totals = list_grads[:, BLK:2 * BLK]
    totals = totals + jnp.concatenate([list_grads[1:, :BLK], zero_block], 0)
    totals = totals + jnp.concatenate([zero_block, list_grads[:-1, 2 * BLK:3 * BLK]], 0)
    partner_terms = to_bf16(list_grads[:, 3 * BLK:])
    totals = totals.at[partners.reshape(-1)].add(partner_terms.reshape(nblocks * R, BLK, DH))
    shards = totals.reshape(N_SEQ, -1, DH)
    shards = shards.at[:, :SUMR].add(summary_grads.reshape(N_SEQ, SUMR, DH))
    return shards.reshape(nblocks, BLK, DH)


def head_grads(query_per_head, key_head, value_per_head, head_gradient, attended_head, partners, allowed, score_scale):
    key_sequence = key_lists(key_head, partners)
    value_sequence = key_lists(value_per_head, partners)
    key_digest = digest_blocks(key_head)
    value_digest = digest_blocks(value_per_head)
    local_probs, distant_probs = probabilities(query_per_head, key_sequence, key_digest, allowed, score_scale)
    local_bias = to_bf16(local_probs)
    distant_bias = to_bf16(distant_probs)
    local_prob_grad = jnp.einsum("gnm,gtm->gnt", head_gradient, value_sequence)
    distant_prob_grad = jnp.einsum("mfp,jp->mfj", head_gradient, value_digest)
    offset = jnp.sum(head_gradient * attended_head, -1)[..., None]
    local_score_grad = to_bf16(local_probs * (local_prob_grad - offset) * score_scale)
    distant_score_grad = to_bf16(distant_probs * (distant_prob_grad - offset) * score_scale)
    query_gradient = jnp.einsum("teh,thz->tez", local_score_grad, key_sequence) + jnp.einsum("umj,jc->umc", distant_score_grad, key_digest)
    local_key_grad = jnp.einsum("sfv,sfz->svz", local_score_grad, query_per_head)
    local_value_grad = jnp.einsum("sfv,sfz->svz", local_bias, head_gradient)
    distant_key_grad = jnp.einsum("ngm,ngz->mz", distant_score_grad, query_per_head)
    distant_value_grad = jnp.einsum("ngm,ngz->mz", distant_bias, head_gradient)
    return query_gradient, place_grads(local_key_grad, distant_key_grad, partners), place_grads(local_value_grad, distant_value_grad, partners)


def reference(queries, keys, values, partners, out_weight, grad_out):
    length = queries.shape[0]
    nblocks = length // BLK
    score_scale = DH ** -0.5
    allowed = window_mask(nblocks)

    def split_heads(tensor):
        return tensor.astype(jnp.float32).reshape(nblocks, BLK, H, DH).transpose(2, 0, 1, 3)

    def join_heads(tensor):
        return tensor.transpose(1, 2, 0, 3).reshape(length, D).astype(jnp.bfloat16)

    query_heads = split_heads(queries)
    key_heads = split_heads(keys)
    value_heads = split_heads(values)

    def forward(parts):
        return attend_head(parts[0], parts[1], parts[2], partners, allowed, score_scale)

    attended = join_heads(lax.map(forward, (query_heads, key_heads, value_heads)))
    mixed = jnp.dot(attended, out_weight, preferred_element_type=jnp.float32).astype(jnp.bfloat16)
    grad_attended = jnp.dot(grad_out, out_weight.T, preferred_element_type=jnp.float32).astype(jnp.bfloat16)
    grad_weight = jnp.dot(attended.T, grad_out, preferred_element_type=jnp.float32)

    def backward(parts):
        return head_grads(parts[0], parts[1], parts[2], parts[3], parts[4], partners, allowed, score_scale)

    query_gradient, grad_k, grad_v = lax.map(backward, (query_heads, key_heads, value_heads, split_heads(grad_attended), split_heads(attended)))
    return mixed, join_heads(query_gradient), join_heads(grad_k), join_heads(grad_v), grad_weight
```

```python
import functools

import jax
import jax.numpy as jnp
from jax import lax
from jax.experimental import pallas as pl
from jax.experimental.pallas import tpu as pltpu
from jax.sharding import PartitionSpec as P

DH = 64
BLK = 64
R = 3
SUMR = 16
LANES = 128
CHUNKS = 1
VMEM = 48 * 1024 * 1024
F32 = jnp.float32
BF16 = jnp.bfloat16


def pack_kernel(capacity, chunks, asked, k_ref, v_ref, *outs):
    shard = pl.program_id(0)
    width = k_ref.shape[1] // chunks
    for c, out in enumerate(outs):
        cols = slice(c * width, (c + 1) * width)
        for j, src in enumerate((k_ref, v_ref)):
            for n in range(capacity):
                block = jnp.maximum(asked[shard * capacity + n], 0)
                rows = pl.ds(pl.multiple_of(block * BLK, BLK), BLK)
                at = (j * capacity + n) * BLK
                out[0, at : at + BLK, :] = src[rows, cols]
            at = 2 * capacity * BLK + j * SUMR
            out[0, at : at + SUMR, :] = src[0:SUMR, cols]


def attend_kernel(
    capacity, meta, q_ref, k_ref, v_ref, arrived, g_ref, gft_ref,
    att_ref, dq_ref, dk_ref, dv_ref, back, kl, vl, dks, dvs,
):
    shards = arrived.shape[0]
    tokens = q_ref.shape[0]
    blocks = tokens // BLK
    requests = blocks * R
    nsum = shards * SUMR
    near = (3 + R) * BLK
    total = near + nsum
    sum_at = 2 * capacity * BLK
    weight_at = sum_at + 2 * SUMR
    weight_rows = back.shape[1] - weight_at
    first = lax.broadcasted_iota(jnp.int32, (1, LANES), 1) < DH
    place = lax.broadcasted_iota(jnp.int32, (1, total), 1)

    kl[near:, :] = arrived[:, sum_at : sum_at + SUMR, :].reshape(nsum, LANES)
    vl[near:, :] = arrived[:, sum_at + SUMR : sum_at + 2 * SUMR, :].reshape(nsum, LANES)
    dk_ref[...] = jnp.zeros_like(dk_ref)
    dv_ref[...] = jnp.zeros_like(dv_ref)
    dks[...] = jnp.zeros_like(dks)
    dvs[...] = jnp.zeros_like(dvs)

    def both(x):
        zero = jnp.zeros_like(x)
        return jnp.concatenate([jnp.where(first, x, zero), jnp.where(first, zero, x)], 0)

    def merge(x):
        return jnp.where(first, x[:BLK], x[BLK:])

    def step(i, carry):
        row = pl.multiple_of(i * BLK, BLK)
        here = pl.ds(row, BLK)
        window = pl.ds(row, 3 * BLK)
        kl[0 : 3 * BLK, :] = k_ref[window, :]
        vl[0 : 3 * BLK, :] = v_ref[window, :]
        spots = []
        for r in range(R):
            owner = meta[i * R + r]
            rank = meta[requests + i * R + r]
            at_k = pl.ds(pl.multiple_of(rank * BLK, BLK), BLK)
            at_v = pl.ds(pl.multiple_of((capacity + rank) * BLK, BLK), BLK)
            spots.append((owner, at_k, at_v))
            at = (3 + r) * BLK
            kl[at : at + BLK, :] = arrived[owner, at_k, :]
            vl[at : at + BLK, :] = arrived[owner, at_v, :]
        keys = kl[...]
        vals = vl[...]
        qs = both(q_ref[here, :] * jnp.asarray(DH**-0.5, BF16))
        g = g_ref[here, :]
        gs = both(g)
        nt = (((1,), (1,)), ((), ()))
        tn = (((0,), (0,)), ((), ()))
        s = lax.dot_general(qs, keys, nt, preferred_element_type=F32)
        no_left = (i == 0) & (meta[2 * requests] > 0)
        no_right = (i == blocks - 1) & (meta[2 * requests + 1] > 0)
        hidden = ((place < BLK) & no_left) | (
            (place >= 2 * BLK) & (place < 3 * BLK) & no_right
        )
        s = jnp.where(hidden, -1e30, s)
        e = jnp.exp(s - jnp.max(s, -1, keepdims=True))
        p = e * (1.0 / jnp.sum(e, -1, keepdims=True))
        pb = p.astype(BF16)
        o = merge(jnp.dot(pb, vals, preferred_element_type=F32)).astype(BF16)
        att_ref[here, :] = o
        dp = lax.dot_general(gs, vals, nt, preferred_element_type=F32)
        go = both(g.astype(F32) * o.astype(F32))
        delta = jnp.sum(go, -1, keepdims=True)
        ds = (p * (dp - delta)).astype(BF16)
        dq = merge(jnp.dot(ds, keys, preferred_element_type=F32)) * (DH**-0.5)
        dq_ref[here, :] = dq.astype(BF16)
        dkl = lax.dot_general(ds, qs, tn, preferred_element_type=F32)
        dvl = lax.dot_general(pb, gs, tn, preferred_element_type=F32)
        dk_ref[window, :] += dkl[: 3 * BLK]
        dv_ref[window, :] += dvl[: 3 * BLK]
        for r, (owner, at_k, at_v) in enumerate(spots):
            at = (3 + r) * BLK
            back[owner, at_k, :] = dkl[at : at + BLK].astype(BF16)
            back[owner, at_v, :] = dvl[at : at + BLK].astype(BF16)
        dks[...] += dkl[near:]
        dvs[...] += dvl[near:]
        return carry

    lax.fori_loop(0, blocks, step, 0)
    back[:, sum_at : sum_at + SUMR, :] = dks[...].astype(BF16).reshape(shards, SUMR, LANES)
    back[:, sum_at + SUMR : weight_at, :] = dvs[...].astype(BF16).reshape(shards, SUMR, LANES)
    terms = jnp.dot(gft_ref[...], att_ref[...], preferred_element_type=F32)
    back[:, weight_at:, :] = terms.astype(BF16).reshape(shards, weight_rows, LANES)


def combine_kernel(
    capacity, asked, dk_ref, dv_ref, prev_ref, next_ref, back, gk_ref, gv_ref, gw_ref, acc
):
    shards = back.shape[0]
    tokens = gk_ref.shape[0]
    sum_at = 2 * capacity * BLK
    weight_at = sum_at + 2 * SUMR
    for j, (own, out) in enumerate(((dk_ref, gk_ref), (dv_ref, gv_ref))):
        acc[...] = own[BLK : BLK + tokens, :]
        half = slice(j * BLK, (j + 1) * BLK)
        acc[:BLK, :] += prev_ref[half, :].astype(F32)
        acc[tokens - BLK :, :] += next_ref[half, :].astype(F32)
        at = sum_at + j * SUMR
        acc[:SUMR, :] += jnp.sum(back[:, at : at + SUMR, :].astype(F32), 0)

        def add(slot, carry):
            block = asked[slot]

            @pl.when(block >= 0)
            def _():
                rows = pl.ds(pl.multiple_of(block * BLK, BLK), BLK)
                rank = j * capacity + lax.rem(slot, capacity)
                spot = pl.ds(pl.multiple_of(rank * BLK, BLK), BLK)
                acc[rows, :] += back[lax.div(slot, capacity), spot, :].astype(F32)

            return carry

        lax.fori_loop(0, shards * capacity, add, 0)
        out[...] = acc[...].astype(BF16)
    gw_ref[...] = jnp.sum(back[:, weight_at:, :].astype(F32), 0)


def per_device(queries, keys, values, partners, out_weight, grad_out):
    shards = lax.axis_size("seq")
    my_shard = lax.axis_index("seq")
    my_half = lax.axis_index("head")
    tokens, width = queries.shape
    model = out_weight.shape[1]
    blocks = tokens // BLK
    capacity = (R * blocks + shards - 1) // shards
    requests = blocks * R
    chunks = CHUNKS
    cwidth = width // chunks
    pairs = cwidth // LANES
    sent_rows = 2 * capacity * BLK + 2 * SUMR
    back_rows = sent_rows + model // shards
    nsum = shards * SUMR
    total = (3 + R) * BLK + nsum
    up = [(i, i + 1) for i in range(shards - 1)]
    down = [(i + 1, i) for i in range(shards - 1)]
    swap = [(0, 1), (1, 0)]
    params = pltpu.CompilerParams(vmem_limit_bytes=VMEM)

    wanted = partners.reshape(-1)
    owners = wanted // blocks
    inside = wanted % blocks
    order = jnp.arange(requests)
    earlier = (owners[:, None] == owners[None, :]) & (order[None, :] < order[:, None])
    ranks = jnp.sum(earlier.astype(jnp.int32), 1)
    slots = owners * capacity + ranks
    hits = (slots[:, None] == jnp.arange(shards * capacity)[None, :]).astype(jnp.int32)
    asks = (jnp.sum(hits * (inside[:, None] + 1), 0) - 1).reshape(shards, capacity)
    asked = lax.all_to_all(asks, "seq", split_axis=0, concat_axis=0, tiled=True).reshape(-1)
    ends = jnp.stack([my_shard == 0, my_shard == shards - 1]).astype(jnp.int32)
    meta = jnp.concatenate([owners, ranks, ends])

    whole = pl.BlockSpec((tokens, width), lambda s, m: (0, 0))
    sent = pl.pallas_call(
        functools.partial(pack_kernel, capacity, chunks),
        out_shape=[jax.ShapeDtypeStruct((shards, sent_rows, cwidth), BF16)] * chunks,
        grid_spec=pltpu.PrefetchScalarGridSpec(
            num_scalar_prefetch=1,
            grid=(shards,),
            in_specs=[whole, whole],
            out_specs=[pl.BlockSpec((1, sent_rows, cwidth), lambda s, m: (s, 0, 0))] * chunks,
        ),
        compiler_params=params,
        name="pack",
    )(asked, keys, values)
    arrived = [
        lax.all_to_all(x, "seq", split_axis=0, concat_axis=0, tiled=True) for x in sent
    ]

    tail = jnp.concatenate([keys[tokens - BLK :], values[tokens - BLK :]], 0)
    lead = jnp.concatenate([keys[:BLK], values[:BLK]], 0)
    before = lax.ppermute(tail, "seq", up)
    after = lax.ppermute(lead, "seq", down)
    k_pad = jnp.concatenate([before[:BLK], keys, after[:BLK]], 0)
    v_pad = jnp.concatenate([before[BLK:], values, after[BLK:]], 0)
    grad_full = lax.all_gather(grad_out, "head", axis=0, tiled=True)
    weight_other = lax.ppermute(out_weight, "head", swap)
    grad_attended = lax.dot_general(
        grad_full, out_weight, (((1,), (1,)), ((), ())), preferred_element_type=F32
    ).astype(BF16)
    grad_turned = grad_full.T

    results = []
    for c in range(chunks):
        column = lambda p, m, c=c: (0, c * pairs + p)
        local = lambda p, m: (0, p)
        local3 = lambda p, m: (0, 0, p)
        results.append(
            pl.pallas_call(
                functools.partial(attend_kernel, capacity),
                out_shape=[
                    jax.ShapeDtypeStruct((tokens, cwidth), BF16),
                    jax.ShapeDtypeStruct((tokens, cwidth), BF16),
                    jax.ShapeDtypeStruct((tokens + 2 * BLK, cwidth), F32),
                    jax.ShapeDtypeStruct((tokens + 2 * BLK, cwidth), F32),
                    jax.ShapeDtypeStruct((shards, back_rows, cwidth), BF16),
                ],
                grid_spec=pltpu.PrefetchScalarGridSpec(
                    num_scalar_prefetch=1,
                    grid=(pairs,),
                    in_specs=[
                        pl.BlockSpec((tokens, LANES), column),
                        pl.BlockSpec((tokens + 2 * BLK, LANES), column),
                        pl.BlockSpec((tokens + 2 * BLK, LANES), column),
                        pl.BlockSpec((shards, sent_rows, LANES), local3),
                        pl.BlockSpec((tokens, LANES), column),
                        pl.BlockSpec((model, tokens), lambda p, m: (0, 0)),
                    ],
                    out_specs=[
                        pl.BlockSpec((tokens, LANES), local),
                        pl.BlockSpec((tokens, LANES), local),
                        pl.BlockSpec((tokens + 2 * BLK, LANES), local),
                        pl.BlockSpec((tokens + 2 * BLK, LANES), local),
                        pl.BlockSpec((shards, back_rows, LANES), local3),
                    ],
                    scratch_shapes=[
                        pltpu.VMEM((total, LANES), BF16),
                        pltpu.VMEM((total, LANES), BF16),
                        pltpu.VMEM((nsum, LANES), F32),
                        pltpu.VMEM((nsum, LANES), F32),
                    ],
                ),
                compiler_params=params,
                cost_estimate=pl.CostEstimate(
                    flops=12 * tokens * total * LANES * pairs * 4,
                    bytes_accessed=8 * tokens * cwidth * 2,
                    transcendentals=tokens * total * 2 * pairs,
                ),
                name="attend",
            )(meta, queries, k_pad, v_pad, arrived[c], grad_attended, grad_turned)
        )

    finals = []
    for c in range(chunks):
        dk, dv, back = results[c][2:]
        returned = lax.all_to_all(back, "seq", split_axis=0, concat_axis=0, tiled=True)
        to_prev = jnp.concatenate([dk[:BLK], dv[:BLK]], 0).astype(BF16)
        to_next = jnp.concatenate([dk[tokens + BLK :], dv[tokens + BLK :]], 0).astype(BF16)
        from_next = lax.ppermute(to_prev, "seq", down)
        from_prev = lax.ppermute(to_next, "seq", up)
        local = lambda p, m: (0, p)
        finals.append(
            pl.pallas_call(
                functools.partial(combine_kernel, capacity),
                out_shape=[
                    jax.ShapeDtypeStruct((tokens, cwidth), BF16),
                    jax.ShapeDtypeStruct((tokens, cwidth), BF16),
                    jax.ShapeDtypeStruct((model // shards, cwidth), F32),
                ],
                grid_spec=pltpu.PrefetchScalarGridSpec(
                    num_scalar_prefetch=1,
                    grid=(pairs,),
                    in_specs=[
                        pl.BlockSpec((tokens + 2 * BLK, LANES), local),
                        pl.BlockSpec((tokens + 2 * BLK, LANES), local),
                        pl.BlockSpec((2 * BLK, LANES), local),
                        pl.BlockSpec((2 * BLK, LANES), local),
                        pl.BlockSpec((shards, back_rows, LANES), lambda p, m: (0, 0, p)),
                    ],
                    out_specs=[
                        pl.BlockSpec((tokens, LANES), local),
                        pl.BlockSpec((tokens, LANES), local),
                        pl.BlockSpec((model // shards, LANES), local),
                    ],
                    scratch_shapes=[pltpu.VMEM((tokens, LANES), F32)],
                ),
                compiler_params=params,
                name="combine",
            )(asked, dk, dv, from_prev, from_next, returned)
        )

    def join(parts):
        return parts[0] if chunks == 1 else jnp.concatenate(parts, 1)

    attended = join([r[0] for r in results])
    half = tokens // 2
    mine = lax.dynamic_slice_in_dim(attended, my_half * half, half, 0)
    others = lax.dynamic_slice_in_dim(attended, (1 - my_half) * half, half, 0)
    received = lax.ppermute(others, "head", swap)
    mixed = jnp.dot(mine, out_weight, preferred_element_type=F32) + jnp.dot(
        received, weight_other, preferred_element_type=F32
    )
    return (
        mixed.astype(BF16),
        join([r[1] for r in results]),
        join([f[0] for f in finals]),
        join([f[1] for f in finals]),
        join([f[2] for f in finals]).T,
    )


def solution(mesh):
    in_specs = (
        P("seq", "head"),
        P("seq", "head"),
        P("seq", "head"),
        P("seq", None),
        P("head", None),
        P(("seq", "head"), None),
    )
    out_specs = (
        P(("seq", "head"), None),
        P("seq", "head"),
        P("seq", "head"),
        P("seq", "head"),
        P("head", "seq"),
    )
    return jax.shard_map(
        per_device, mesh=mesh, in_specs=in_specs, out_specs=out_specs, check_vma=False
    )
```

```python
import functools

import jax
import jax.numpy as jnp
from jax import lax
from jax.experimental import pallas as pl
from jax.experimental.pallas import tpu as pltpu
from jax.sharding import PartitionSpec as P

DH = 64
BLK = 64
R = 3
SUMR = 16
LANES = 128
VMEM = 58 * 1024 * 1024
F32 = jnp.float32
BF16 = jnp.bfloat16

MESH = pl.DeviceIdType.MESH


def pack_kernel(capacity, asked, k_ref, v_ref, out):
    shard = pl.program_id(0)
    for c in range(out.shape[0]):
        cols = slice(c * LANES, (c + 1) * LANES)
        for j, src in enumerate((k_ref, v_ref)):
            for n in range(capacity):
                block = jnp.maximum(asked[shard * capacity + n], 0)
                rows = pl.ds(pl.multiple_of(block * BLK, BLK), BLK)
                at = (j * capacity + n) * BLK
                out[c, 0, at : at + BLK, :] = src[rows, cols]
            at = 2 * capacity * BLK + j * SUMR
            out[c, 0, at : at + SUMR, :] = src[0:SUMR, cols]


def attend_kernel(
    shards, capacity,
    meta, q_ref, w_ref, wo_ref, k_hbm, v_hbm, go_hbm, sent,
    mixed_ref, dq_ref, dk_ref, dv_ref, returned, halo_in,
    kpad, vpad, gf, g_all, att, received, arrived, cur_k, cur_v, part_k, part_v, back, halo_out,
    kl, vl, dka, dva, dks, dvs,
    local_sem, halo_send, halo_recv, go_send, go_recv, out_send, out_recv,
    ret_send, ret_recv, edge_send, edge_recv, att_send, att_recv,
):
    tokens, width = q_ref.shape
    model = w_ref.shape[1]
    half = tokens // 2
    blocks = tokens // BLK
    pairs = width // LANES
    requests = blocks * R
    nsum = shards * SUMR
    near = (3 + R) * BLK
    total = near + nsum
    sum_at = 2 * capacity * BLK
    weight_at = sum_at + 2 * SUMR
    weight_rows = model // shards
    me = lax.axis_index("seq")
    side = lax.axis_index("head")
    after = lax.rem(me + 1, shards)
    before = lax.rem(me + shards - 1, shards)
    other = 1 - side
    first = lax.broadcasted_iota(jnp.int32, (1, LANES), 1) < DH
    place = lax.broadcasted_iota(jnp.int32, (1, total), 1)
    nt = (((1,), (1,)), ((), ()))
    tn = (((0,), (0,)), ((), ()))

    barrier = pltpu.get_barrier_semaphore()

    def greet(k, carry):
        pl.semaphore_signal(
            barrier, inc=1, device_id={"seq": lax.rem(me + k, shards)}, device_id_type=MESH
        )
        return carry

    lax.fori_loop(1, shards, greet, 0)
    pl.semaphore_signal(barrier, inc=1, device_id={"head": other}, device_id_type=MESH)
    pl.semaphore_wait(barrier, shards)

    def remote(src, dst, send, recv, to):
        return pltpu.make_async_remote_copy(
            src_ref=src, dst_ref=dst, send_sem=send, recv_sem=recv,
            device_id=to, device_id_type=MESH,
        )

    middle = pl.ds(BLK, tokens)
    near_copies = [
        remote(k_hbm.at[pl.ds(tokens - BLK, BLK)], kpad.at[pl.ds(0, BLK)],
               halo_send.at[0], halo_recv.at[0], {"seq": after}),
        remote(k_hbm.at[pl.ds(0, BLK)], kpad.at[pl.ds(BLK + tokens, BLK)],
               halo_send.at[1], halo_recv.at[1], {"seq": before}),
        remote(v_hbm.at[pl.ds(tokens - BLK, BLK)], vpad.at[pl.ds(0, BLK)],
               halo_send.at[2], halo_recv.at[2], {"seq": after}),
        remote(v_hbm.at[pl.ds(0, BLK)], vpad.at[pl.ds(BLK + tokens, BLK)],
               halo_send.at[3], halo_recv.at[3], {"seq": before}),
    ]
    my_rows = pl.ds(pl.multiple_of(side * half, half), half)
    other_rows = pl.ds(pl.multiple_of(other * half, half), half)
    go_copy = remote(go_hbm, gf.at[my_rows], go_send, go_recv, {"head": other})
    own_copies = [
        pltpu.make_async_copy(k_hbm, kpad.at[middle], local_sem.at[0]),
        pltpu.make_async_copy(v_hbm, vpad.at[middle], local_sem.at[1]),
        pltpu.make_async_copy(go_hbm, gf.at[my_rows], local_sem.at[2]),
    ]
    for copy in near_copies + [go_copy] + own_copies:
        copy.start()

    def send_pair(c, carry):
        def send(k, carry):
            to = lax.rem(me + k, shards)
            remote(sent.at[c, to], arrived.at[c, me], out_send.at[c, k], out_recv.at[c, k],
                   {"seq": to}).start()
            return carry

        lax.fori_loop(1, shards, send, 0)
        pltpu.make_async_copy(sent.at[c, me], arrived.at[c, me], out_recv.at[c, 0]).start()
        return carry

    lax.fori_loop(0, pairs, send_pair, 0)

    for copy in own_copies + [go_copy]:
        copy.wait()

    def project(j, carry):
        rows = pl.ds(pl.multiple_of(j * 256, 256), 256)
        g_all[rows, :] = lax.dot_general(
            gf[rows, :], w_ref[...], nt, preferred_element_type=F32
        ).astype(BF16)
        return carry

    lax.fori_loop(0, tokens // 256, project, 0)
    for copy in near_copies:
        copy.wait()

    def both(x):
        zero = jnp.zeros_like(x)
        return jnp.concatenate([jnp.where(first, x, zero), jnp.where(first, zero, x)], 0)

    def merge(x):
        return jnp.where(first, x[:BLK], x[BLK:])

    def edge_copies(c):
        return [
            remote(halo_out.at[c, 1], halo_in.at[c, 0], edge_send.at[c, 0], edge_recv.at[c, 0],
                   {"seq": after}),
            remote(halo_out.at[c, 0], halo_in.at[c, 1], edge_send.at[c, 1], edge_recv.at[c, 1],
                   {"seq": before}),
        ]

    def att_copy(c):
        return remote(att.at[c, other_rows], received.at[c], att_send.at[c], att_recv.at[c],
                      {"head": other})

    def pair(c, carry):
        cols = pl.ds(pl.multiple_of(c * LANES, LANES), LANES)

        def landed(k, carry):
            source = lax.rem(me + shards - k, shards)
            remote(sent.at[c, source], arrived.at[c, source], out_send.at[c, k],
                   out_recv.at[c, k], {"seq": source}).wait_recv()
            return carry

        lax.fori_loop(1, shards, landed, 0)
        pltpu.make_async_copy(sent.at[c, me], arrived.at[c, me], out_recv.at[c, 0]).wait()

        def take(d, carry):
            for n in range(capacity):
                at = n * BLK
                cur_k[d * capacity + n] = arrived[c, d, at : at + BLK, :]
                at = (capacity + n) * BLK
                cur_v[d * capacity + n] = arrived[c, d, at : at + BLK, :]
            return carry

        lax.fori_loop(0, shards, take, 0)
        kl[near:, :] = arrived[c, :, sum_at : sum_at + SUMR, :].reshape(nsum, LANES)
        vl[near:, :] = arrived[c, :, sum_at + SUMR : weight_at, :].reshape(nsum, LANES)
        for ref in (dka, dva, dks, dvs):
            ref[...] = jnp.zeros_like(ref)

        def step(i, carry):
            row = pl.multiple_of(i * BLK, BLK)
            here = pl.ds(row, BLK)
            window = pl.ds(row, 3 * BLK)
            kl[0 : 3 * BLK, :] = kpad[window, cols]
            vl[0 : 3 * BLK, :] = vpad[window, cols]
            for r in range(R):
                slot = meta[i * R + r]
                at = (3 + r) * BLK
                kl[at : at + BLK, :] = cur_k[slot]
                vl[at : at + BLK, :] = cur_v[slot]
            keys = kl[...]
            vals = vl[...]
            qs = both(q_ref[here, cols] * jnp.asarray(DH**-0.5, BF16))
            g = g_all[here, cols]
            gs = both(g)
            s = lax.dot_general(qs, keys, nt, preferred_element_type=F32)
            no_left = (i == 0) & (me == 0)
            no_right = (i == blocks - 1) & (me == shards - 1)
            hidden = ((place < BLK) & no_left) | (
                (place >= 2 * BLK) & (place < 3 * BLK) & no_right
            )
            s = jnp.where(hidden, -1e30, s)
            e = jnp.exp(s - jnp.max(s, -1, keepdims=True))
            p = e * (1.0 / jnp.sum(e, -1, keepdims=True))
            pb = p.astype(BF16)
            o = merge(jnp.dot(pb, vals, preferred_element_type=F32)).astype(BF16)
            att[c, here, :] = o
            dp = lax.dot_general(gs, vals, nt, preferred_element_type=F32)
            delta = jnp.sum(both(g.astype(F32) * o.astype(F32)), -1, keepdims=True)
            ds = (p * (dp - delta)).astype(BF16)
            dq = merge(jnp.dot(ds, keys, preferred_element_type=F32)) * (DH**-0.5)
            dq_ref[here, cols] = dq.astype(BF16)
            dkl = lax.dot_general(ds, qs, tn, preferred_element_type=F32)
            dvl = lax.dot_general(pb, gs, tn, preferred_element_type=F32)
            dka[window, :] += dkl[: 3 * BLK]
            dva[window, :] += dvl[: 3 * BLK]
            for r in range(R):
                at = (3 + r) * BLK
                part_k[i * R + r] = dkl[at : at + BLK].astype(BF16)
                part_v[i * R + r] = dvl[at : at + BLK].astype(BF16)
            dks[...] += dkl[near:]
            dvs[...] += dvl[near:]
            return carry

        lax.fori_loop(0, blocks, step, 0)
        att_copy(c).start()

        def fill(d, carry):
            for n in range(capacity):
                request = meta[requests + d * capacity + n]
                at = n * BLK
                back[c, d, at : at + BLK, :] = part_k[request]
                at = (capacity + n) * BLK
                back[c, d, at : at + BLK, :] = part_v[request]
            return carry

        lax.fori_loop(0, shards, fill, 0)
        back[c, :, sum_at : sum_at + SUMR, :] = (
            dks[...].astype(BF16).reshape(shards, SUMR, LANES)
        )
        back[c, :, sum_at + SUMR : weight_at, :] = (
            dvs[...].astype(BF16).reshape(shards, SUMR, LANES)
        )
        count = 256 // weight_rows

        def weigh(j, carry):
            columns = pl.ds(pl.multiple_of(j * 256, 256), 256)
            terms = lax.dot_general(gf[:, columns], att[c], tn, preferred_element_type=F32)
            back[c, pl.ds(j * count, count), weight_at:, :] = terms.astype(BF16).reshape(
                count, weight_rows, LANES
            )
            return carry

        lax.fori_loop(0, model // 256, weigh, 0)

        def send(k, carry):
            to = lax.rem(me + k, shards)
            remote(back.at[c, to], returned.at[c, me], ret_send.at[c, k], ret_recv.at[c, k],
                   {"seq": to}).start()
            return carry

        lax.fori_loop(1, shards, send, 0)
        pltpu.make_async_copy(back.at[c, me], returned.at[c, me], ret_recv.at[c, 0]).start()
        dk_ref[:, cols] = dka[BLK : BLK + tokens, :]
        dv_ref[:, cols] = dva[BLK : BLK + tokens, :]
        halo_out[c, 0, :BLK, :] = dka[:BLK, :].astype(BF16)
        halo_out[c, 0, BLK:, :] = dva[:BLK, :].astype(BF16)
        halo_out[c, 1, :BLK, :] = dka[BLK + tokens :, :].astype(BF16)
        halo_out[c, 1, BLK:, :] = dva[BLK + tokens :, :].astype(BF16)
        for copy in edge_copies(c):
            copy.start()
        return carry

    lax.fori_loop(0, pairs, pair, 0)

    def swapped(c, carry):
        att_copy(c).wait()
        return carry

    lax.fori_loop(0, pairs, swapped, 0)

    def mix(j, carry):
        rows = pl.ds(pl.multiple_of(j * LANES, LANES), LANES)
        own = pl.ds(pl.multiple_of(side * half + j * LANES, LANES), LANES)
        mine = jnp.concatenate([att[c, own, :] for c in range(pairs)], 1)
        theirs = jnp.concatenate([received[c, rows, :] for c in range(pairs)], 1)
        mixed = jnp.dot(mine, w_ref[...], preferred_element_type=F32)
        mixed = mixed + jnp.dot(theirs, wo_ref[...], preferred_element_type=F32)
        mixed_ref[rows, :] = mixed.astype(BF16)
        return carry

    lax.fori_loop(0, half // LANES, mix, 0)

    def finish(c, carry):
        def done(k, carry):
            to = lax.rem(me + k, shards)
            source = lax.rem(me + shards - k, shards)
            remote(sent.at[c, to], arrived.at[c, me], out_send.at[c, k], out_recv.at[c, k],
                   {"seq": to}).wait_send()
            remote(back.at[c, to], returned.at[c, me], ret_send.at[c, k], ret_recv.at[c, k],
                   {"seq": to}).wait_send()
            remote(back.at[c, source], returned.at[c, source], ret_send.at[c, k],
                   ret_recv.at[c, k], {"seq": source}).wait_recv()
            return carry

        lax.fori_loop(1, shards, done, 0)
        pltpu.make_async_copy(back.at[c, me], returned.at[c, me], ret_recv.at[c, 0]).wait()
        for copy in edge_copies(c):
            copy.wait()
        return carry

    lax.fori_loop(0, pairs, finish, 0)


def combine_kernel(capacity, asked, dk_ref, dv_ref, halo, back, gk_ref, gv_ref, gw_ref, acc):
    shards = back.shape[1]
    tokens = gk_ref.shape[0]
    sum_at = 2 * capacity * BLK
    weight_at = sum_at + 2 * SUMR
    for j, (own, out) in enumerate(((dk_ref, gk_ref), (dv_ref, gv_ref))):
        acc[...] = own[...]
        side = slice(j * BLK, (j + 1) * BLK)
        acc[:BLK, :] += halo[0, 0, side, :].astype(F32)
        acc[tokens - BLK :, :] += halo[0, 1, side, :].astype(F32)
        at = sum_at + j * SUMR
        acc[:SUMR, :] += jnp.sum(back[0, :, at : at + SUMR, :].astype(F32), 0)

        def add(shard, carry):
            for n in range(capacity):
                block = asked[shard * capacity + n]
                spot = slice((j * capacity + n) * BLK, (j * capacity + n + 1) * BLK)

                @pl.when(block >= 0)
                def _():
                    rows = pl.ds(pl.multiple_of(block * BLK, BLK), BLK)
                    acc[rows, :] += back[0, shard, spot, :].astype(F32)

            return carry

        lax.fori_loop(0, shards, add, 0)
        out[...] = acc[...].astype(BF16)
    gw_ref[...] = jnp.sum(back[0, :, weight_at:, :].astype(F32), 0)


def per_device(queries, keys, values, partners, out_weight, grad_out):
    shards = lax.axis_size("seq")
    tokens, width = queries.shape
    model = out_weight.shape[1]
    half = tokens // 2
    blocks = tokens // BLK
    capacity = (R * blocks + shards - 1) // shards
    requests = blocks * R
    pairs = width // LANES
    sent_rows = 2 * capacity * BLK + 2 * SUMR
    back_rows = sent_rows + model // shards
    nsum = shards * SUMR
    total = (3 + R) * BLK + nsum
    params = pltpu.CompilerParams(vmem_limit_bytes=VMEM)

    wanted = partners.reshape(-1)
    owners = wanted // blocks
    inside = wanted % blocks
    order = jnp.arange(requests)
    earlier = (owners[:, None] == owners[None, :]) & (order[None, :] < order[:, None])
    ranks = jnp.sum(earlier.astype(jnp.int32), 1)
    slots = owners * capacity + ranks
    hits = (slots[:, None] == jnp.arange(shards * capacity)[None, :]).astype(jnp.int32)
    asks = (jnp.sum(hits * (inside[:, None] + 1), 0) - 1).reshape(shards, capacity)
    asked = lax.all_to_all(asks, "seq", split_axis=0, concat_axis=0, tiled=True).reshape(-1)
    weight_other = lax.ppermute(out_weight, "head", [(0, 1), (1, 0)])
    fillers = jnp.sum(hits * order[:, None], 0)
    meta = jnp.concatenate([slots, fillers])

    whole = pl.BlockSpec((tokens, width), lambda s, m: (0, 0))
    sent = pl.pallas_call(
        functools.partial(pack_kernel, capacity),
        out_shape=jax.ShapeDtypeStruct((pairs, shards, sent_rows, LANES), BF16),
        grid_spec=pltpu.PrefetchScalarGridSpec(
            num_scalar_prefetch=1,
            grid=(shards,),
            in_specs=[whole, whole],
            out_specs=pl.BlockSpec((pairs, 1, sent_rows, LANES), lambda s, m: (0, s, 0, 0)),
        ),
        compiler_params=params,
        name="pack",
    )(asked, keys, values)

    vmem = pl.BlockSpec(memory_space=pltpu.VMEM)
    anywhere = pl.BlockSpec(memory_space=pl.ANY)
    sems = pltpu.SemaphoreType.DMA
    mixed, grad_queries, dk, dv, returned, halo = pl.pallas_call(
        functools.partial(attend_kernel, shards, capacity),
        out_shape=[
            jax.ShapeDtypeStruct((half, model), BF16),
            jax.ShapeDtypeStruct((tokens, width), BF16),
            jax.ShapeDtypeStruct((tokens, width), F32),
            jax.ShapeDtypeStruct((tokens, width), F32),
            jax.ShapeDtypeStruct((pairs, shards, back_rows, LANES), BF16),
            jax.ShapeDtypeStruct((pairs, 2, 2 * BLK, LANES), BF16),
        ],
        in_specs=[pl.BlockSpec(memory_space=pltpu.SMEM), vmem, vmem, vmem]
        + [anywhere] * 4,
        out_specs=[vmem] * 4 + [anywhere] * 2,
        scratch_shapes=[
            pltpu.VMEM((tokens + 2 * BLK, width), BF16),
            pltpu.VMEM((tokens + 2 * BLK, width), BF16),
            pltpu.VMEM((tokens, model), BF16),
            pltpu.VMEM((tokens, width), BF16),
            pltpu.VMEM((pairs, tokens, LANES), BF16),
            pltpu.VMEM((pairs, half, LANES), BF16),
            pltpu.VMEM((pairs, shards, sent_rows, LANES), BF16),
            pltpu.VMEM((shards * capacity, BLK, LANES), BF16),
            pltpu.VMEM((shards * capacity, BLK, LANES), BF16),
            pltpu.VMEM((requests, BLK, LANES), BF16),
            pltpu.VMEM((requests, BLK, LANES), BF16),
            pltpu.VMEM((pairs, shards, back_rows, LANES), BF16),
            pltpu.VMEM((pairs, 2, 2 * BLK, LANES), BF16),
            pltpu.VMEM((total, LANES), BF16),
            pltpu.VMEM((total, LANES), BF16),
            pltpu.VMEM((tokens + 2 * BLK, LANES), F32),
            pltpu.VMEM((tokens + 2 * BLK, LANES), F32),
            pltpu.VMEM((nsum, LANES), F32),
            pltpu.VMEM((nsum, LANES), F32),
            sems((3,)), sems((4,)), sems((4,)), sems, sems,
            sems((pairs, shards)), sems((pairs, shards)),
            sems((pairs, shards)), sems((pairs, shards)),
            sems((pairs, 2)), sems((pairs, 2)), sems((pairs,)), sems((pairs,)),
        ],
        compiler_params=pltpu.CompilerParams(
            vmem_limit_bytes=VMEM, collective_id=0, has_side_effects=True
        ),
        name="attend",
    )(meta, queries, out_weight, weight_other, keys, values, grad_out, sent)

    local = lambda p, m: (0, p)
    local4 = lambda p, m: (p, 0, 0, 0)
    grad_keys, grad_values, grad_weight = pl.pallas_call(
        functools.partial(combine_kernel, capacity),
        out_shape=[
            jax.ShapeDtypeStruct((tokens, width), BF16),
            jax.ShapeDtypeStruct((tokens, width), BF16),
            jax.ShapeDtypeStruct((model // shards, width), F32),
        ],
        grid_spec=pltpu.PrefetchScalarGridSpec(
            num_scalar_prefetch=1,
            grid=(pairs,),
            in_specs=[
                pl.BlockSpec((tokens, LANES), local),
                pl.BlockSpec((tokens, LANES), local),
                pl.BlockSpec((1, 2, 2 * BLK, LANES), local4),
                pl.BlockSpec((1, shards, back_rows, LANES), local4),
            ],
            out_specs=[
                pl.BlockSpec((tokens, LANES), local),
                pl.BlockSpec((tokens, LANES), local),
                pl.BlockSpec((model // shards, LANES), local),
            ],
            scratch_shapes=[pltpu.VMEM((tokens, LANES), F32)],
        ),
        compiler_params=params,
        name="combine",
    )(asked, dk, dv, halo, returned)
    return (mixed, grad_queries, grad_keys, grad_values, grad_weight.T)


def solution(mesh):
    in_specs = (
        P("seq", "head"),
        P("seq", "head"),
        P("seq", "head"),
        P("seq", None),
        P("head", None),
        P(("seq", "head"), None),
    )
    out_specs = (
        P(("seq", "head"), None),
        P("seq", "head"),
        P("seq", "head"),
        P("seq", "head"),
        P("head", "seq"),
    )
    return jax.shard_map(
        per_device, mesh=mesh, in_specs=in_specs, out_specs=out_specs, check_vma=False
    )
```

```python
import functools

import jax
import jax.numpy as jnp
from jax import lax
from jax.experimental import pallas as pl
from jax.experimental.pallas import tpu as pltpu
from jax.sharding import PartitionSpec as P

DH = 64
BLK = 64
R = 3
SUMR = 16
GROUP = 4
LANES = 128
VMEM = 58 * 1024 * 1024
F32 = jnp.float32
BF16 = jnp.bfloat16

MESH = pl.DeviceIdType.MESH


def pack_kernel(capacity, asked, k_ref, v_ref, out):
    shard = pl.program_id(0)
    for c in range(out.shape[0]):
        cols = slice(c * LANES, (c + 1) * LANES)
        for j, src in enumerate((k_ref, v_ref)):
            for n in range(capacity):
                block = jnp.maximum(asked[shard * capacity + n], 0)
                rows = pl.ds(pl.multiple_of(block * BLK, BLK), BLK)
                at = (j * capacity + n) * BLK
                out[c, 0, at : at + BLK, :] = src[rows, cols]
            at = 2 * capacity * BLK + j * SUMR
            out[c, 0, at : at + SUMR, :] = src[0:SUMR, cols]


def attend_kernel(
    shards, capacity,
    meta, q_ref, w_ref, wo_ref, k_hbm, v_hbm, go_hbm, sent,
    mixed_ref, dq_ref, dk_ref, dv_ref, returned, halo_in, terms_in,
    kpad, vpad, gf, g_all, att, received, arrived, cur_k, cur_v, part_k, part_v, back, halo_out,
    terms, group_in, group_sum,
    kl, vl, dka, dva, dks, dvs,
    local_sem, halo_send, halo_recv, go_send, go_recv, out_send, out_recv,
    ret_send, ret_recv, edge_send, edge_recv, att_send, att_recv,
    group_send, group_recv, terms_send, terms_recv,
):
    tokens, width = q_ref.shape
    model = w_ref.shape[1]
    half = tokens // 2
    blocks = tokens // BLK
    pairs = width // LANES
    requests = blocks * R
    nsum = shards * SUMR
    near = (3 + R) * BLK
    total = near + nsum
    sum_at = 2 * capacity * BLK
    weight_at = sum_at + 2 * SUMR
    weight_rows = model // shards
    me = lax.axis_index("seq")
    groups = shards // GROUP
    group = me // GROUP
    seat = lax.rem(me, GROUP)
    side = lax.axis_index("head")
    after = lax.rem(me + 1, shards)
    before = lax.rem(me + shards - 1, shards)
    other = 1 - side
    first = lax.broadcasted_iota(jnp.int32, (1, LANES), 1) < DH
    place = lax.broadcasted_iota(jnp.int32, (1, total), 1)
    nt = (((1,), (1,)), ((), ()))
    tn = (((0,), (0,)), ((), ()))

    barrier = pltpu.get_barrier_semaphore()

    def greet(k, carry):
        pl.semaphore_signal(
            barrier, inc=1, device_id={"seq": lax.rem(me + k, shards)}, device_id_type=MESH
        )
        return carry

    lax.fori_loop(1, shards, greet, 0)
    pl.semaphore_signal(barrier, inc=1, device_id={"head": other}, device_id_type=MESH)
    pl.semaphore_wait(barrier, shards)

    def remote(src, dst, send, recv, to):
        return pltpu.make_async_remote_copy(
            src_ref=src, dst_ref=dst, send_sem=send, recv_sem=recv,
            device_id=to, device_id_type=MESH,
        )

    middle = pl.ds(BLK, tokens)
    near_copies = [
        remote(k_hbm.at[pl.ds(tokens - BLK, BLK)], kpad.at[pl.ds(0, BLK)],
               halo_send.at[0], halo_recv.at[0], {"seq": after}),
        remote(k_hbm.at[pl.ds(0, BLK)], kpad.at[pl.ds(BLK + tokens, BLK)],
               halo_send.at[1], halo_recv.at[1], {"seq": before}),
        remote(v_hbm.at[pl.ds(tokens - BLK, BLK)], vpad.at[pl.ds(0, BLK)],
               halo_send.at[2], halo_recv.at[2], {"seq": after}),
        remote(v_hbm.at[pl.ds(0, BLK)], vpad.at[pl.ds(BLK + tokens, BLK)],
               halo_send.at[3], halo_recv.at[3], {"seq": before}),
    ]
    my_rows = pl.ds(pl.multiple_of(side * half, half), half)
    other_rows = pl.ds(pl.multiple_of(other * half, half), half)
    go_copy = remote(go_hbm, gf.at[my_rows], go_send, go_recv, {"head": other})
    own_copies = [
        pltpu.make_async_copy(k_hbm, kpad.at[middle], local_sem.at[0]),
        pltpu.make_async_copy(v_hbm, vpad.at[middle], local_sem.at[1]),
        pltpu.make_async_copy(go_hbm, gf.at[my_rows], local_sem.at[2]),
    ]
    for copy in near_copies + [go_copy] + own_copies:
        copy.start()

    def send_pair(c, carry):
        def send(k, carry):
            to = lax.rem(me + k, shards)
            remote(sent.at[c, to], arrived.at[c, me], out_send.at[c, k], out_recv.at[c, k],
                   {"seq": to}).start()
            return carry

        lax.fori_loop(1, shards, send, 0)
        pltpu.make_async_copy(sent.at[c, me], arrived.at[c, me], out_recv.at[c, 0]).start()
        return carry

    lax.fori_loop(0, pairs, send_pair, 0)

    for copy in own_copies + [go_copy]:
        copy.wait()

    def project(j, carry):
        rows = pl.ds(pl.multiple_of(j * 256, 256), 256)
        g_all[rows, :] = lax.dot_general(
            gf[rows, :], w_ref[...], nt, preferred_element_type=F32
        ).astype(BF16)
        return carry

    lax.fori_loop(0, tokens // 256, project, 0)
    for copy in near_copies:
        copy.wait()

    def both(x):
        zero = jnp.zeros_like(x)
        return jnp.concatenate([jnp.where(first, x, zero), jnp.where(first, zero, x)], 0)

    def merge(x):
        return jnp.where(first, x[:BLK], x[BLK:])

    def edge_copies(c):
        return [
            remote(halo_out.at[c, 1], halo_in.at[c, 0], edge_send.at[c, 0], edge_recv.at[c, 0],
                   {"seq": after}),
            remote(halo_out.at[c, 0], halo_in.at[c, 1], edge_send.at[c, 1], edge_recv.at[c, 1],
                   {"seq": before}),
        ]

    def att_copy(c):
        return remote(att.at[c, other_rows], received.at[c], att_send.at[c], att_recv.at[c],
                      {"head": other})

    def group_copy(c, k):
        mate = lax.rem(seat + k, GROUP)
        return remote(terms.at[c, mate], group_in.at[c, seat], group_send.at[c, k],
                      group_recv.at[c, k], {"seq": group * GROUP + mate})

    def group_arrival(c, k):
        mate = lax.rem(seat + GROUP - k, GROUP)
        return remote(terms.at[c, mate], group_in.at[c, mate], group_send.at[c, k],
                      group_recv.at[c, k], {"seq": group * GROUP + mate})

    def terms_copy(c, k):
        there = lax.rem(group + k, groups)
        return remote(group_sum.at[c, there], terms_in.at[c, group], terms_send.at[c, k],
                      terms_recv.at[c, k], {"seq": there * GROUP + seat})

    def terms_arrival(c, k):
        there = lax.rem(group + groups - k, groups)
        return remote(group_sum.at[c, there], terms_in.at[c, there], terms_send.at[c, k],
                      terms_recv.at[c, k], {"seq": there * GROUP + seat})

    def own_terms(c):
        return pltpu.make_async_copy(
            group_sum.at[c, group], terms_in.at[c, group], terms_recv.at[c, 0]
        )

    def pair(c, carry):
        cols = pl.ds(pl.multiple_of(c * LANES, LANES), LANES)

        def landed(k, carry):
            source = lax.rem(me + shards - k, shards)
            remote(sent.at[c, source], arrived.at[c, source], out_send.at[c, k],
                   out_recv.at[c, k], {"seq": source}).wait_recv()
            return carry

        lax.fori_loop(1, shards, landed, 0)
        pltpu.make_async_copy(sent.at[c, me], arrived.at[c, me], out_recv.at[c, 0]).wait()

        def take(d, carry):
            for n in range(capacity):
                at = n * BLK
                cur_k[d * capacity + n] = arrived[c, d, at : at + BLK, :]
                at = (capacity + n) * BLK
                cur_v[d * capacity + n] = arrived[c, d, at : at + BLK, :]
            return carry

        lax.fori_loop(0, shards, take, 0)
        kl[near:, :] = arrived[c, :, sum_at : sum_at + SUMR, :].reshape(nsum, LANES)
        vl[near:, :] = arrived[c, :, sum_at + SUMR : weight_at, :].reshape(nsum, LANES)
        for ref in (dka, dva, dks, dvs):
            ref[...] = jnp.zeros_like(ref)

        def step(i, carry):
            row = pl.multiple_of(i * BLK, BLK)
            here = pl.ds(row, BLK)
            window = pl.ds(row, 3 * BLK)
            kl[0 : 3 * BLK, :] = kpad[window, cols]
            vl[0 : 3 * BLK, :] = vpad[window, cols]
            for r in range(R):
                slot = meta[i * R + r]
                at = (3 + r) * BLK
                kl[at : at + BLK, :] = cur_k[slot]
                vl[at : at + BLK, :] = cur_v[slot]
            keys = kl[...]
            vals = vl[...]
            qs = both(q_ref[here, cols] * jnp.asarray(DH**-0.5, BF16))
            g = g_all[here, cols]
            gs = both(g)
            s = lax.dot_general(qs, keys, nt, preferred_element_type=F32)
            no_left = (i == 0) & (me == 0)
            no_right = (i == blocks - 1) & (me == shards - 1)
            hidden = ((place < BLK) & no_left) | (
                (place >= 2 * BLK) & (place < 3 * BLK) & no_right
            )
            s = jnp.where(hidden, -1e30, s)
            e = jnp.exp(s - jnp.max(s, -1, keepdims=True))
            p = e * (1.0 / jnp.sum(e, -1, keepdims=True))
            pb = p.astype(BF16)
            o = merge(jnp.dot(pb, vals, preferred_element_type=F32)).astype(BF16)
            att[c, here, :] = o
            dp = lax.dot_general(gs, vals, nt, preferred_element_type=F32)
            delta = jnp.sum(both(g.astype(F32) * o.astype(F32)), -1, keepdims=True)
            ds = (p * (dp - delta)).astype(BF16)
            dq = merge(jnp.dot(ds, keys, preferred_element_type=F32)) * (DH**-0.5)
            dq_ref[here, cols] = dq.astype(BF16)
            dkl = lax.dot_general(ds, qs, tn, preferred_element_type=F32)
            dvl = lax.dot_general(pb, gs, tn, preferred_element_type=F32)
            dka[window, :] += dkl[: 3 * BLK]
            dva[window, :] += dvl[: 3 * BLK]
            for r in range(R):
                at = (3 + r) * BLK
                part_k[i * R + r] = dkl[at : at + BLK].astype(BF16)
                part_v[i * R + r] = dvl[at : at + BLK].astype(BF16)
            dks[...] += dkl[near:]
            dvs[...] += dvl[near:]
            return carry

        lax.fori_loop(0, blocks, step, 0)
        att_copy(c).start()

        for n, ref in enumerate((dks, dvs)):
            sums = ref[...].astype(BF16).reshape(groups, GROUP, SUMR, LANES)
            for q in range(GROUP):
                terms[c, q, :, n * SUMR : (n + 1) * SUMR, :] = sums[:, q]
        count = 256 // (weight_rows * GROUP)

        def weigh(j, carry):
            columns = pl.ds(pl.multiple_of(j * 256, 256), 256)
            product = lax.dot_general(gf[:, columns], att[c], tn, preferred_element_type=F32)
            product = product.astype(BF16).reshape(count, GROUP, weight_rows, LANES)
            for q in range(GROUP):
                terms[c, q, pl.ds(j * count, count), 2 * SUMR :, :] = product[:, q]
            return carry

        lax.fori_loop(0, model // 256, weigh, 0)
        for k in range(1, GROUP):
            group_copy(c, k).start()

        def fill(d, carry):
            for n in range(capacity):
                request = meta[requests + d * capacity + n]
                at = n * BLK
                back[c, d, at : at + BLK, :] = part_k[request]
                at = (capacity + n) * BLK
                back[c, d, at : at + BLK, :] = part_v[request]
            return carry

        lax.fori_loop(0, shards, fill, 0)

        def send(k, carry):
            to = lax.rem(me + k, shards)
            remote(back.at[c, to], returned.at[c, me], ret_send.at[c, k], ret_recv.at[c, k],
                   {"seq": to}).start()
            return carry

        lax.fori_loop(1, shards, send, 0)
        pltpu.make_async_copy(back.at[c, me], returned.at[c, me], ret_recv.at[c, 0]).start()
        dk_ref[:, cols] = dka[BLK : BLK + tokens, :]
        dv_ref[:, cols] = dva[BLK : BLK + tokens, :]
        halo_out[c, 0, :BLK, :] = dka[:BLK, :].astype(BF16)
        halo_out[c, 0, BLK:, :] = dva[:BLK, :].astype(BF16)
        halo_out[c, 1, :BLK, :] = dka[BLK + tokens :, :].astype(BF16)
        halo_out[c, 1, BLK:, :] = dva[BLK + tokens :, :].astype(BF16)
        for copy in edge_copies(c):
            copy.start()
        return carry

    lax.fori_loop(0, pairs, pair, 0)

    def add_up(c, carry):
        for k in range(1, GROUP):
            group_arrival(c, k).wait_recv()

        def add(z, carry):
            value = terms[c, seat, z].astype(F32)
            for k in range(1, GROUP):
                value = value + group_in[c, lax.rem(seat + k, GROUP), z].astype(F32)
            group_sum[c, z] = value.astype(BF16)
            return carry

        lax.fori_loop(0, groups, add, 0)

        def send(k, carry):
            terms_copy(c, k).start()
            return carry

        lax.fori_loop(1, groups, send, 0)
        own_terms(c).start()
        return carry

    lax.fori_loop(0, pairs, add_up, 0)

    def swapped(c, carry):
        att_copy(c).wait()
        return carry

    lax.fori_loop(0, pairs, swapped, 0)

    def mix(j, carry):
        rows = pl.ds(pl.multiple_of(j * LANES, LANES), LANES)
        own = pl.ds(pl.multiple_of(side * half + j * LANES, LANES), LANES)
        mine = jnp.concatenate([att[c, own, :] for c in range(pairs)], 1)
        theirs = jnp.concatenate([received[c, rows, :] for c in range(pairs)], 1)
        mixed = jnp.dot(mine, w_ref[...], preferred_element_type=F32)
        mixed = mixed + jnp.dot(theirs, wo_ref[...], preferred_element_type=F32)
        mixed_ref[rows, :] = mixed.astype(BF16)
        return carry

    lax.fori_loop(0, half // LANES, mix, 0)

    def finish(c, carry):
        def done(k, carry):
            to = lax.rem(me + k, shards)
            source = lax.rem(me + shards - k, shards)
            remote(sent.at[c, to], arrived.at[c, me], out_send.at[c, k], out_recv.at[c, k],
                   {"seq": to}).wait_send()
            remote(back.at[c, to], returned.at[c, me], ret_send.at[c, k], ret_recv.at[c, k],
                   {"seq": to}).wait_send()
            remote(back.at[c, source], returned.at[c, source], ret_send.at[c, k],
                   ret_recv.at[c, k], {"seq": source}).wait_recv()
            return carry

        lax.fori_loop(1, shards, done, 0)
        pltpu.make_async_copy(back.at[c, me], returned.at[c, me], ret_recv.at[c, 0]).wait()
        for copy in edge_copies(c):
            copy.wait()
        for k in range(1, GROUP):
            group_copy(c, k).wait_send()

        def summed(k, carry):
            terms_copy(c, k).wait_send()
            terms_arrival(c, k).wait_recv()
            return carry

        lax.fori_loop(1, groups, summed, 0)
        own_terms(c).wait()
        return carry

    lax.fori_loop(0, pairs, finish, 0)


def combine_kernel(capacity, asked, dk_ref, dv_ref, halo, back, terms, gk_ref, gv_ref, gw_ref, acc):
    shards = back.shape[1]
    tokens = gk_ref.shape[0]
    for j, (own, out) in enumerate(((dk_ref, gk_ref), (dv_ref, gv_ref))):
        acc[...] = own[...]
        side = slice(j * BLK, (j + 1) * BLK)
        acc[:BLK, :] += halo[0, 0, side, :].astype(F32)
        acc[tokens - BLK :, :] += halo[0, 1, side, :].astype(F32)
        at = j * SUMR
        acc[:SUMR, :] += jnp.sum(terms[0, :, at : at + SUMR, :].astype(F32), 0)

        def add(shard, carry):
            for n in range(capacity):
                block = asked[shard * capacity + n]
                spot = slice((j * capacity + n) * BLK, (j * capacity + n + 1) * BLK)

                @pl.when(block >= 0)
                def _():
                    rows = pl.ds(pl.multiple_of(block * BLK, BLK), BLK)
                    acc[rows, :] += back[0, shard, spot, :].astype(F32)

            return carry

        lax.fori_loop(0, shards, add, 0)
        out[...] = acc[...].astype(BF16)
    gw_ref[...] = jnp.sum(terms[0, :, 2 * SUMR :, :].astype(F32), 0)


def per_device(queries, keys, values, partners, out_weight, grad_out):
    shards = lax.axis_size("seq")
    tokens, width = queries.shape
    model = out_weight.shape[1]
    half = tokens // 2
    blocks = tokens // BLK
    capacity = (R * blocks + shards - 1) // shards
    requests = blocks * R
    pairs = width // LANES
    sent_rows = 2 * capacity * BLK + 2 * SUMR
    back_rows = 2 * capacity * BLK
    groups = shards // GROUP
    term_rows = 2 * SUMR + model // shards
    nsum = shards * SUMR
    total = (3 + R) * BLK + nsum
    params = pltpu.CompilerParams(vmem_limit_bytes=VMEM)

    wanted = partners.reshape(-1)
    owners = wanted // blocks
    inside = wanted % blocks
    order = jnp.arange(requests)
    earlier = (owners[:, None] == owners[None, :]) & (order[None, :] < order[:, None])
    ranks = jnp.sum(earlier.astype(jnp.int32), 1)
    slots = owners * capacity + ranks
    hits = (slots[:, None] == jnp.arange(shards * capacity)[None, :]).astype(jnp.int32)
    asks = (jnp.sum(hits * (inside[:, None] + 1), 0) - 1).reshape(shards, capacity)
    asked = lax.all_to_all(asks, "seq", split_axis=0, concat_axis=0, tiled=True).reshape(-1)
    weight_other = lax.ppermute(out_weight, "head", [(0, 1), (1, 0)])
    fillers = jnp.sum(hits * order[:, None], 0)
    meta = jnp.concatenate([slots, fillers])

    whole = pl.BlockSpec((tokens, width), lambda s, m: (0, 0))
    sent = pl.pallas_call(
        functools.partial(pack_kernel, capacity),
        out_shape=jax.ShapeDtypeStruct((pairs, shards, sent_rows, LANES), BF16),
        grid_spec=pltpu.PrefetchScalarGridSpec(
            num_scalar_prefetch=1,
            grid=(shards,),
            in_specs=[whole, whole],
            out_specs=pl.BlockSpec((pairs, 1, sent_rows, LANES), lambda s, m: (0, s, 0, 0)),
        ),
        compiler_params=params,
        name="pack",
    )(asked, keys, values)

    vmem = pl.BlockSpec(memory_space=pltpu.VMEM)
    anywhere = pl.BlockSpec(memory_space=pl.ANY)
    sems = pltpu.SemaphoreType.DMA
    mixed, grad_queries, dk, dv, returned, halo, terms = pl.pallas_call(
        functools.partial(attend_kernel, shards, capacity),
        out_shape=[
            jax.ShapeDtypeStruct((half, model), BF16),
            jax.ShapeDtypeStruct((tokens, width), BF16),
            jax.ShapeDtypeStruct((tokens, width), F32),
            jax.ShapeDtypeStruct((tokens, width), F32),
            jax.ShapeDtypeStruct((pairs, shards, back_rows, LANES), BF16),
            jax.ShapeDtypeStruct((pairs, 2, 2 * BLK, LANES), BF16),
            jax.ShapeDtypeStruct((pairs, groups, term_rows, LANES), BF16),
        ],
        in_specs=[pl.BlockSpec(memory_space=pltpu.SMEM), vmem, vmem, vmem]
        + [anywhere] * 4,
        out_specs=[vmem] * 4 + [anywhere] * 3,
        scratch_shapes=[
            pltpu.VMEM((tokens + 2 * BLK, width), BF16),
            pltpu.VMEM((tokens + 2 * BLK, width), BF16),
            pltpu.VMEM((tokens, model), BF16),
            pltpu.VMEM((tokens, width), BF16),
            pltpu.VMEM((pairs, tokens, LANES), BF16),
            pltpu.VMEM((pairs, half, LANES), BF16),
            pltpu.VMEM((pairs, shards, sent_rows, LANES), BF16),
            pltpu.VMEM((shards * capacity, BLK, LANES), BF16),
            pltpu.VMEM((shards * capacity, BLK, LANES), BF16),
            pltpu.VMEM((requests, BLK, LANES), BF16),
            pltpu.VMEM((requests, BLK, LANES), BF16),
            pltpu.VMEM((pairs, shards, back_rows, LANES), BF16),
            pltpu.VMEM((pairs, 2, 2 * BLK, LANES), BF16),
            pltpu.VMEM((pairs, GROUP, groups, term_rows, LANES), BF16),
            pltpu.VMEM((pairs, GROUP, groups, term_rows, LANES), BF16),
            pltpu.VMEM((pairs, groups, term_rows, LANES), BF16),
            pltpu.VMEM((total, LANES), BF16),
            pltpu.VMEM((total, LANES), BF16),
            pltpu.VMEM((tokens + 2 * BLK, LANES), F32),
            pltpu.VMEM((tokens + 2 * BLK, LANES), F32),
            pltpu.VMEM((nsum, LANES), F32),
            pltpu.VMEM((nsum, LANES), F32),
            sems((3,)), sems((4,)), sems((4,)), sems, sems,
            sems((pairs, shards)), sems((pairs, shards)),
            sems((pairs, shards)), sems((pairs, shards)),
            sems((pairs, 2)), sems((pairs, 2)), sems((pairs,)), sems((pairs,)),
            sems((pairs, GROUP)), sems((pairs, GROUP)),
            sems((pairs, groups)), sems((pairs, groups)),
        ],
        compiler_params=pltpu.CompilerParams(
            vmem_limit_bytes=VMEM, collective_id=0, has_side_effects=True
        ),
        name="attend",
    )(meta, queries, out_weight, weight_other, keys, values, grad_out, sent)

    local = lambda p, m: (0, p)
    local4 = lambda p, m: (p, 0, 0, 0)
    grad_keys, grad_values, grad_weight = pl.pallas_call(
        functools.partial(combine_kernel, capacity),
        out_shape=[
            jax.ShapeDtypeStruct((tokens, width), BF16),
            jax.ShapeDtypeStruct((tokens, width), BF16),
            jax.ShapeDtypeStruct((model // shards, width), F32),
        ],
        grid_spec=pltpu.PrefetchScalarGridSpec(
            num_scalar_prefetch=1,
            grid=(pairs,),
            in_specs=[
                pl.BlockSpec((tokens, LANES), local),
                pl.BlockSpec((tokens, LANES), local),
                pl.BlockSpec((1, 2, 2 * BLK, LANES), local4),
                pl.BlockSpec((1, shards, back_rows, LANES), local4),
                pl.BlockSpec((1, groups, term_rows, LANES), local4),
            ],
            out_specs=[
                pl.BlockSpec((tokens, LANES), local),
                pl.BlockSpec((tokens, LANES), local),
                pl.BlockSpec((model // shards, LANES), local),
            ],
            scratch_shapes=[pltpu.VMEM((tokens, LANES), F32)],
        ),
        compiler_params=params,
        name="combine",
    )(asked, dk, dv, halo, returned, terms)
    return (mixed, grad_queries, grad_keys, grad_values, grad_weight.T)


def solution(mesh):
    in_specs = (
        P("seq", "head"),
        P("seq", "head"),
        P("seq", "head"),
        P("seq", None),
        P("head", None),
        P(("seq", "head"), None),
    )
    out_specs = (
        P(("seq", "head"), None),
        P("seq", "head"),
        P("seq", "head"),
        P("seq", "head"),
        P("head", "seq"),
    )
    return jax.shard_map(
        per_device, mesh=mesh, in_specs=in_specs, out_specs=out_specs, check_vma=False
    )
```
